32 devices in a mesh: row: 8 (over z, y), col: 4 (over x, core).
Axes of the slice: x: 2, y: 2, z: 4, core: 2. Of those that a mesh axis runs over, the one named last changes fastest.
Arguments:
- a_blocks: float32 [128, 8, 125, 125], P('row', 'col'), may hold values from -0.1875 to 0.1875
- a_pattern: int32 [128, 8], P('row', 'col'), may hold values 0 or 1
- row_owner: int32 [128], replicated, may hold values from 0 to 127, as said below
- prolong: float32 [8, 24, 125, 125], P('row', 'col'), may hold values from -6 to 6
- p_pattern: int32 [8, 24], P('row', 'col'), may hold values 0 or 1
- prolong_slab: float32 [128, 8, 125, 125], P('row'), may hold values from -0.0625 to 0.0625
Outputs:
- coarse: float32 [8, 24, 125, 125], P('row', 'col')
The draws below stay inside these ranges and needn't reach their ends.
Inputs may be any that keep to these rules, and one draw needn't show every extreme that they name: row_owner is a permutation; the 16 element-order rows e with e // 16 equal go to at most 2 positions p of any one value p // 16, and exactly 2 for each value they reach.
All inputs are finite; a program needn't handle non-finite values. No bound on the sum of `a_pattern` or of `p_pattern` on one device may be relied on, other than what follows from the above.
Results may differ from the reference program's by a relative error of at most 0.0001.
Values sent between devices are 32-bit elements; how exact they have to be, the bound alone decides.
A program may use at most 128 MiB of HBM per device.

```python
import jax
import jax.numpy as jnp
from jax import lax

B = 125
MB = 16
CAP = 2
FINE = 128
K = 8
NC = 24
NA = 8
N_ROW = 8


def draw_row_owner(key, part):
    count = FINE // MB
    first_key, second_key = jax.random.split(key)
    sigma = jax.random.permutation(first_key, count)
    slot_order = jax.vmap(lambda k: jax.random.permutation(k, MB))(jax.random.split(second_key, count))
    element = jnp.arange(FINE, dtype=jnp.int32)
    source = element // MB
    within = element % MB
    group_idx = within // CAP
    target = sigma[(source + group_idx) % count]
    return (target * MB + slot_order[target, within]).astype(jnp.int32)


def plant(values, own_key, low, top_value):
    shape = values.shape
    index_at = [jax.random.randint(jax.random.fold_in(own_key, axis), (), 0, shape[axis]) for axis in range(len(shape))]
    values = values.at[tuple(index_at)].set(low)
    longest = shape.index(max(shape))
    index_at[longest] = (index_at[longest] + 1) % shape[longest]
    return values.at[tuple(index_at)].set(top_value)


def spiked(entries, rng, source, target, parts, factor):
    owner, partner = [(jnp.arange(entries.shape[axis_at]) // (entries.shape[axis_at] // parts)).reshape([-1 if axis == axis_at else 1 for axis in range(entries.ndim)]) for axis_at in (source, target)]
    chosen = jax.random.permutation(rng, parts)[partner]
    strong = (owner == chosen) | (owner == (partner + parts // 2) % parts)
    return jnp.where(strong, factor * entries, entries)


def block_scale(stream_key, shape, cuts, smallest, top_value):
    def one(axis_at, parts):
        heights = jax.random.uniform(jax.random.fold_in(jax.random.fold_in(stream_key, 6), axis_at), (parts,), jnp.float32, smallest / len(cuts), top_value / len(cuts))
        return jnp.repeat(jnp.exp(heights), shape[axis_at] // parts).reshape((-1,) + (1,) * (len(shape) - axis_at - 1))

    level = one(*cuts[0])
    for cut in cuts[1:]:
        level = level * one(*cut)
    return level


def gaussian(rng, shape, width, most, cuts=(), kind=jnp.bfloat16):
    array = jax.random.normal(rng, shape, jnp.float32) * width
    if len(cuts) > 0:
        array = block_scale(rng, shape, cuts, -0.22, 0.18) * array
    return jnp.clip(array, min=-most, max=most).astype(kind)


def gaussian_with(stream_key, shape, width, reach, cuts, heavy, kind=jnp.bfloat16):
    entries = width * jax.random.normal(stream_key, shape, jnp.float32)
    if cuts:
        entries = entries * block_scale(stream_key, shape, cuts, -0.22, 0.18)
    return jnp.clip(spiked(entries, jax.random.fold_in(stream_key, 3), *heavy), -reach, reach).astype(kind)


def setup_inputs(seed: int = 0) -> dict:
    seeds = jax.random.split(jax.random.key(seed), 7)
    return {
        "a_blocks": gaussian(seeds[0], (FINE, K, B, B), (B * K) ** -0.5, 0.1875, ((0, 8), (1, 4)), jnp.float32),
        "a_pattern": plant((jax.random.randint(seeds[1], (FINE, K), 0, 2) < 1).astype(jnp.int32), jax.random.fold_in(seeds[1], 1), 0, 1),
        "row_owner": draw_row_owner(jax.random.fold_in(seeds[6], 71), 0),
        "prolong": gaussian(seeds[3], (K, NC, B, B), 1.0, 6.0, ((0, 8), (1, 4)), jnp.float32),
        "p_pattern": plant((jax.random.randint(seeds[4], (K, NC), 0, 2) < 1).astype(jnp.int32), jax.random.fold_in(seeds[4], 1), 0, 1),
        "prolong_slab": gaussian_with(seeds[5], (FINE, NA, B, B), (B * FINE) ** -0.5, 0.0625, ((0, 8),), (0, 1, 8, 2.0), jnp.float32),
    }


def reference(a_blocks, a_pattern, row_owner, prolong, p_pattern, prolong_slab):
    masked = a_blocks * a_pattern.astype(a_blocks.dtype)[:, :, None, None]
    grid_a = jnp.zeros_like(masked).at[row_owner.astype(jnp.int32)].set(masked)
    p_masked = prolong * p_pattern.astype(prolong.dtype)[:, :, None, None]
    grouped_a = grid_a.reshape((N_ROW, MB) + grid_a.shape[1:])
    grouped_slab = prolong_slab.reshape((N_ROW, MB) + prolong_slab.shape[1:])

    def one_group(total, pieces):
        rows_a, rows_slab = pieces
        product = jnp.einsum("mkxy,knyz->mnxz", rows_a, p_masked, precision=lax.Precision.HIGHEST)
        return total + jnp.einsum("maxy,mnxz->anyz", rows_slab, product, precision=lax.Precision.HIGHEST), None

    start = jnp.zeros((NA, NC, B, B), dtype=a_blocks.dtype)
    coarse, _ = lax.scan(one_group, start, (grouped_a, grouped_slab))
    return coarse
```

```python
import jax
import jax.numpy as jnp
from jax import lax
from jax.sharding import PartitionSpec as P

CAP = 2


def ranks_of(targets):
    width = targets.shape[-1]
    same = targets[..., :, None] == targets[..., None, :]
    lower = jnp.arange(width)[:, None] > jnp.arange(width)[None, :]
    return jnp.sum(jnp.where(same & lower, 1, 0), axis=-1).astype(jnp.int32)


def pick(rows, at):
    return jnp.stack([lax.dynamic_index_in_dim(rows, at[i], 0, keepdims=False) for i in range(at.shape[0])])


def shards(a_blocks, a_pattern, row_owner, prolong, p_pattern, prolong_slab):
    width = a_blocks.shape[0]
    count = lax.axis_size("row")
    me = lax.axis_index("row")
    masked = a_blocks * a_pattern.astype(jnp.float32)[:, :, None, None]
    p_masked = prolong * p_pattern.astype(jnp.float32)[:, :, None, None]
    p_full = lax.all_gather(p_masked, "row", axis=0, tiled=True)

    table = row_owner.reshape(count, width)
    ranks = ranks_of(table // width)
    targets = lax.dynamic_index_in_dim(table, me, 0, keepdims=False) // width
    mine = lax.dynamic_index_in_dim(ranks, me, 0, keepdims=False)
    slot = targets * CAP + mine
    hit = slot[None, :] == jnp.arange(count * CAP, dtype=jnp.int32)[:, None]
    order = jnp.sum(jnp.where(hit, jnp.arange(width, dtype=jnp.int32)[None, :], 0), axis=1)
    packed = pick(masked, order)
    packed = packed.reshape((count, CAP) + masked.shape[1:])
    received = lax.all_to_all(packed, "row", split_axis=0, concat_axis=0, tiled=True)
    received = received.reshape((count * CAP,) + masked.shape[1:])
    wanted = table[None] == (me * width + jnp.arange(width, dtype=jnp.int32))[:, None, None]
    source = jnp.arange(count, dtype=jnp.int32)[:, None] * CAP + ranks
    where = jnp.sum(jnp.where(wanted, source[None], 0), axis=(1, 2))
    grid_a = pick(received, where)
    part = jnp.einsum(
        "maxy,mkxz->akyz",
        prolong_slab,
        grid_a,
        precision=lax.Precision.HIGH,
        preferred_element_type=jnp.float32,
    )
    mine = lax.psum_scatter(part, "row", scatter_dimension=0, tiled=True)
    mid = lax.all_gather(mine, "col", axis=1, tiled=True)
    return jnp.einsum(
        "akyx,knxz->anyz",
        mid,
        p_full,
        precision=lax.Precision.HIGH,
        preferred_element_type=jnp.float32,
    )


def solution(mesh):
    in_specs = (
        P("row", "col", None, None),
        P("row", "col"),
        P(),
        P("row", "col", None, None),
        P("row", "col"),
        P("row", None, None, None),
    )
    out_specs = P("row", "col", None, None)
    return jax.shard_map(shards, mesh=mesh, in_specs=in_specs, out_specs=out_specs, check_vma=False)
```

```python
import functools

import jax
import jax.numpy as jnp
from jax import lax
from jax.experimental import pallas as pl
from jax.experimental.pallas import tpu as pltpu
from jax.sharding import PartitionSpec as P

CAP = 2
Z = 4
L = 128
MESH = pl.DeviceIdType.MESH


def split(v):
    hi = v.astype(jnp.bfloat16)
    lo = (v - hi.astype(jnp.float32)).astype(jnp.bfloat16)
    return hi, lo


def mul3(ah, al, bh, bl):
    dot = functools.partial(jnp.dot, preferred_element_type=jnp.float32)
    return dot(ah, bh) + (dot(ah, bl) + dot(al, bh))


def kernel(
    R, C, a_hbm, s_hbm, p_in, owner, a_pat, p_pat, out,
    a_v, s_v, asend, arecv, stage, sh, sl, ath, atl, macc, mrecv, mfull, mth, mtl, pbuf, ph, plo, total,
    load, a_s, a_r, m_s, m_r, g_s, g_r, u_s, u_r, d_s, d_r, y_s, y_r,
):
    W, KP, B = a_v.shape[0], a_v.shape[1], a_v.shape[2]
    NA, NJ = s_v.shape[1], p_in.shape[1]
    Y = R // Z
    me, col = lax.axis_index("row"), lax.axis_index("col")
    z, y = lax.div(me, Y), lax.rem(me, Y)

    load_a = pltpu.make_async_copy(a_hbm, a_v, load.at[0])
    load_s = pltpu.make_async_copy(s_hbm, s_v, load.at[1])
    load_a.start()
    load_s.start()

    barrier = pltpu.get_barrier_semaphore()
    for i in range(1, R):
        pl.semaphore_signal(barrier, inc=1, device_id={"row": lax.rem(me + i, R)}, device_id_type=MESH)
    for i in range(1, C):
        pl.semaphore_signal(barrier, inc=1, device_id={"col": lax.rem(col + i, C)}, device_id_type=MESH)

    for n in range(NJ):
        pbuf[me, n] = jnp.zeros((L, L), jnp.float32)
        pbuf[me, n, 0:B, 0:B] = p_in[0, n] * p_pat[0, n].astype(jnp.float32)

    pl.semaphore_wait(barrier, R + C - 2)

    def p_copy(slot, target, s_sem, r_sem):
        return pltpu.make_async_remote_copy(
            src_ref=pbuf.at[slot], dst_ref=pbuf.at[slot], send_sem=s_sem, recv_sem=r_sem,
            device_id={"row": target}, device_id_type=MESH,
        )

    def up(t):
        return p_copy((z - t) * Y + y, me + Y, u_s.at[t], u_r.at[t + 1])

    def down(t):
        return p_copy((z + t) * Y + y, me - Y, d_s.at[t], d_r.at[t + 1])

    def across(zo, i):
        return p_copy(zo * Y + y, z * Y + lax.rem(y + i, Y), y_s.at[zo * Y + i], y_r.at[zo * Y + i])

    def hop(t):
        @pl.when(z >= t)
        def _():
            if t > 0:
                p_copy((z - t) * Y + y, me, u_s.at[t], u_r.at[t]).wait_recv()

            @pl.when(z < Z - 1)
            def _():
                up(t).start()

            for i in range(1, Y):
                across(z - t, i).start()

        @pl.when(z + t < Z)
        def _():
            if t > 0:
                p_copy((z + t) * Y + y, me, d_s.at[t], d_r.at[t]).wait_recv()

            @pl.when(z > 0)
            def _():
                down(t).start()

            if t > 0:
                for i in range(1, Y):
                    across(z + t, i).start()

    hop(0)

    def pair(source, target):
        first, last = jnp.int32(W), jnp.int32(-1)
        for e in range(W):
            hit = lax.div(owner[source * W + e], W) == target
            first = jnp.minimum(first, jnp.where(hit, e, W))
            last = jnp.maximum(last, jnp.where(hit, e, -1))
        valid = last >= 0
        return (jnp.where(valid, first, 0), jnp.where(valid, last, 0)), valid

    def a_copy(step):
        return pltpu.make_async_remote_copy(
            src_ref=asend.at[step], dst_ref=arecv.at[step], send_sem=a_s.at[step], recv_sem=a_r.at[step],
            device_id={"row": lax.rem(me + step, R)}, device_id_type=MESH,
        )

    def pack(buf, step):
        rows, valid = pair(me, lax.rem(me + step, R))
        for s in range(CAP):
            for k in range(KP):
                scale = jnp.where(valid, a_pat[rows[s], k], 0).astype(jnp.float32)
                buf[step, s, k] = jnp.zeros((L, L), jnp.float32)
                buf[step, s, k, 0:B, 0:B] = a_v[rows[s], k] * scale

    def step_of(j):
        half = lax.div(j + 1, 2)
        return R // 2 + half * (1 - 2 * lax.rem(j, 2))

    load_a.wait()

    def send_step(j, carry):
        step = step_of(j)
        pack(asend, step)
        a_copy(step).start()
        return carry

    lax.fori_loop(0, R - 1, send_step, 0)
    pack(arecv, 0)
    stage[...] = jnp.zeros_like(stage)
    macc[...] = jnp.zeros_like(macc)
    load_s.wait()

    def work(step, arrives):
        source = lax.rem(me - step + R, R)
        rows, valid = pair(source, me)
        for s in range(CAP):
            g = jnp.where(valid, owner[source * W + rows[s]] - me * W, 0)

            def slab(b, carry):
                for h in range(2):
                    stage[2 * b + h, 0:B, 0:B] = s_v[g, 2 * b + h]
                for h in range(2):
                    hi, lo = split(stage[2 * b + h])
                    sh[b, s * L : (s + 1) * L, h * L : (h + 1) * L] = hi
                    sl[b, s * L : (s + 1) * L, h * L : (h + 1) * L] = lo
                return carry

            lax.fori_loop(0, NA // 2, slab, 0)
        if arrives:
            a_copy(step).wait_recv()
        for s in range(CAP):
            for k in range(KP):
                hi, lo = split(arecv[step, s, k].T)
                ath[k * L : (k + 1) * L, s * L : (s + 1) * L] = hi
                atl[k * L : (k + 1) * L, s * L : (s + 1) * L] = lo

        def add(b, carry):
            r = mul3(ath[...], atl[...], sh[b], sl[b])
            macc[2 * b] += r[:, 0:L]
            macc[2 * b + 1] += r[:, L : 2 * L]
            return carry

        lax.fori_loop(0, NA // 2, add, 0)

    def remote_step(j, carry):
        work(step_of(j), True)
        return carry

    work(0, False)
    at = 0
    for t in range(1, Z):
        hop(t)
        until = (R - 1) * t // Z if t < Z - 1 else R - 1
        lax.fori_loop(at, until, remote_step, 0)
        at = until

    def m_copy(step):
        target = lax.rem(me + step, R)
        return pltpu.make_async_remote_copy(
            src_ref=macc.at[target], dst_ref=mrecv.at[step], send_sem=m_s.at[step], recv_sem=m_r.at[step],
            device_id={"row": target}, device_id_type=MESH,
        )

    def m_send(j, carry):
        m_copy(step_of(j)).start()
        return carry

    lax.fori_loop(0, R - 1, m_send, 0)

    for zo in range(Z):
        for i in range(1, Y):
            across(zo, i).wait_recv()

    def p_split(r, carry):
        for n in range(NJ):
            hi, lo = split(pbuf[r, n])
            at = pl.ds(pl.multiple_of(r * L, L), L)
            ph[at, n * L : (n + 1) * L] = hi
            plo[at, n * L : (n + 1) * L] = lo
        return carry

    lax.fori_loop(0, R, p_split, 0)

    mfull[col] = macc[me]

    def m_add(j, carry):
        step = step_of(j)
        m_copy(step).wait_recv()
        mfull[col] += mrecv[step]
        return carry

    lax.fori_loop(0, R - 1, m_add, 0)

    def g_copy(i):
        return pltpu.make_async_remote_copy(
            src_ref=mfull.at[col], dst_ref=mfull.at[col], send_sem=g_s.at[i], recv_sem=g_r.at[i],
            device_id={"col": lax.rem(col + i, C)}, device_id_type=MESH,
        )

    for i in range(1, C):
        g_copy(i).start()
    total[...] = jnp.zeros_like(total)

    for i in range(C):
        source = lax.rem(col - i + C, C)
        if i > 0:
            g_copy(i).wait_recv()
        for k in range(KP):
            hi, lo = split(mfull[source, k * L : (k + 1) * L, :].T)
            mth[:, k * L : (k + 1) * L] = hi
            mtl[:, k * L : (k + 1) * L] = lo
        rows = pl.ds(pl.multiple_of(source * KP * L, KP * L), KP * L)
        total[...] += mul3(mth[...], mtl[...], ph[rows, :], plo[rows, :])

    for n in range(NJ):
        out[0, n] = total[0:B, n * L : n * L + B]

    def a_done(j, carry):
        a_copy(j + 1).wait_send()
        m_copy(j + 1).wait_send()
        return carry

    lax.fori_loop(0, R - 1, a_done, 0)
    for i in range(1, C):
        g_copy(i).wait_send()
    for t in range(Z):
        @pl.when((z >= t) & (z < Z - 1))
        def _():
            up(t).wait_send()

        @pl.when((z + t < Z) & (z > 0))
        def _():
            down(t).wait_send()

    for zo in range(Z):
        for i in range(1, Y):
            across(zo, i).wait_send()


def shards(a_blocks, a_pattern, row_owner, prolong, p_pattern, prolong_slab):
    R, C = lax.axis_size("row"), lax.axis_size("col")
    W, KP, B = a_blocks.shape[:3]
    NA, NJ = prolong_slab.shape[1], prolong.shape[1]
    f32, bf16 = jnp.float32, jnp.bfloat16
    dma = pltpu.SemaphoreType.DMA
    vmem = pl.BlockSpec(memory_space=pltpu.VMEM)
    smem = pl.BlockSpec(memory_space=pltpu.SMEM)
    hbm = pl.BlockSpec(memory_space=pl.ANY)
    return pl.pallas_call(
        functools.partial(kernel, R, C),
        out_shape=jax.ShapeDtypeStruct((1, NJ, B, B), f32),
        in_specs=[hbm, hbm, vmem, smem, smem, smem],
        out_specs=vmem,
        scratch_shapes=[
            pltpu.VMEM((W, KP, B, B), f32),
            pltpu.VMEM((W, NA, B, B), f32),
            pltpu.VMEM((R, CAP, KP, L, L), f32),
            pltpu.VMEM((R, CAP, KP, L, L), f32),
            pltpu.VMEM((NA, L, L), f32),
            pltpu.VMEM((NA // 2, CAP * L, 2 * L), bf16),
            pltpu.VMEM((NA // 2, CAP * L, 2 * L), bf16),
            pltpu.VMEM((KP * L, CAP * L), bf16),
            pltpu.VMEM((KP * L, CAP * L), bf16),
            pltpu.VMEM((NA, KP * L, L), f32),
            pltpu.VMEM((R, KP * L, L), f32),
            pltpu.VMEM((C, KP * L, L), f32),
            pltpu.VMEM((L, KP * L), bf16),
            pltpu.VMEM((L, KP * L), bf16),
            pltpu.VMEM((R, NJ, L, L), f32),
            pltpu.VMEM((R * L, NJ * L), bf16),
            pltpu.VMEM((R * L, NJ * L), bf16),
            pltpu.VMEM((L, NJ * L), f32),
            dma((2,)),
            dma((R,)), dma((R,)), dma((R,)), dma((R,)), dma((C,)), dma((C,)),
            dma((Z,)), dma((Z + 1,)), dma((Z,)), dma((Z + 1,)), dma((R,)), dma((R,)),
        ],
        compiler_params=pltpu.CompilerParams(
            collective_id=0, has_side_effects=True, vmem_limit_bytes=58 * 1024 * 1024
        ),
    )(a_blocks, prolong_slab, prolong, row_owner, a_pattern, p_pattern)


def solution(mesh):
    in_specs = (
        P("row", "col", None, None),
        P("row", "col"),
        P(),
        P("row", "col", None, None),
        P("row", "col"),
        P("row", None, None, None),
    )
    out_specs = P("row", "col", None, None)
    return jax.shard_map(shards, mesh=mesh, in_specs=in_specs, out_specs=out_specs, check_vma=False)
```

```python
import functools

import jax
import jax.numpy as jnp
from jax import lax
from jax.experimental import pallas as pl
from jax.experimental.pallas import tpu as pltpu
from jax.sharding import PartitionSpec as P

CAP = 2
Z = 4
L = 128
MESH = pl.DeviceIdType.MESH


def split(v):
    hi = v.astype(jnp.bfloat16)
    lo = (v - hi.astype(jnp.float32)).astype(jnp.bfloat16)
    return hi, lo


def mul3(ah, al, bh, bl):
    dot = functools.partial(jnp.dot, preferred_element_type=jnp.float32)
    return dot(ah, bh) + (dot(ah, bl) + dot(al, bh))


def kernel(
    R, C, a_hbm, s_hbm, p_in, owner, a_pat, p_pat, out,
    a_v, s_v, asend, arecv, stage, sh, sl, ath, atl, macc, mrecv, mfull, mth, mtl, pbuf, ph, plo, total,
    load, a_s, a_r, m_s, m_r, g_s, g_r, u_s, u_r, d_s, d_r, y_s, y_r,
):
    W, KP, B = a_v.shape[0], a_v.shape[1], a_v.shape[2]
    NA, NJ = s_v.shape[1] // B, p_in.shape[1]
    Y = R // Z
    me, col = lax.axis_index("row"), lax.axis_index("col")
    z, y = lax.div(me, Y), lax.rem(me, Y)

    load_a = pltpu.make_async_copy(a_hbm, a_v, load.at[0])
    load_s = pltpu.make_async_copy(s_hbm, s_v, load.at[1])
    load_a.start()
    load_s.start()

    barrier = pltpu.get_barrier_semaphore()
    for i in range(1, R):
        pl.semaphore_signal(barrier, inc=1, device_id={"row": lax.rem(me + i, R)}, device_id_type=MESH)
    for i in range(1, C):
        pl.semaphore_signal(barrier, inc=1, device_id={"col": lax.rem(col + i, C)}, device_id_type=MESH)

    for n in range(NJ):
        pbuf[me, n] = jnp.zeros((L, L), jnp.float32)
        pbuf[me, n, 0:B, 0:B] = p_in[0, n] * p_pat[0, n].astype(jnp.float32)

    pl.semaphore_wait(barrier, R + C - 2)

    def p_copy(slot, target, s_sem, r_sem):
        return pltpu.make_async_remote_copy(
            src_ref=pbuf.at[slot], dst_ref=pbuf.at[slot], send_sem=s_sem, recv_sem=r_sem,
            device_id={"row": target}, device_id_type=MESH,
        )

    def up(t):
        return p_copy((z - t) * Y + y, me + Y, u_s.at[t], u_r.at[t + 1])

    def down(t):
        return p_copy((z + t) * Y + y, me - Y, d_s.at[t], d_r.at[t + 1])

    def across(zo, i):
        return p_copy(zo * Y + y, z * Y + lax.rem(y + i, Y), y_s.at[zo * Y + i], y_r.at[zo * Y + i])

    def hop(t):
        @pl.when(z >= t)
        def _():
            if t > 0:
                p_copy((z - t) * Y + y, me, u_s.at[t], u_r.at[t]).wait_recv()

            @pl.when(z < Z - 1)
            def _():
                up(t).start()

            for i in range(1, Y):
                across(z - t, i).start()

        @pl.when(z + t < Z)
        def _():
            if t > 0:
                p_copy((z + t) * Y + y, me, d_s.at[t], d_r.at[t]).wait_recv()

            @pl.when(z > 0)
            def _():
                down(t).start()

            if t > 0:
                for i in range(1, Y):
                    across(z + t, i).start()

    hop(0)

    def pair(source, target):
        first, last = jnp.int32(W), jnp.int32(-1)
        for e in range(W):
            hit = lax.div(owner[source * W + e], W) == target
            first = jnp.minimum(first, jnp.where(hit, e, W))
            last = jnp.maximum(last, jnp.where(hit, e, -1))
        valid = last >= 0
        return (jnp.where(valid, first, 0), jnp.where(valid, last, 0)), valid

    def a_copy(step):
        return pltpu.make_async_remote_copy(
            src_ref=asend.at[step], dst_ref=arecv.at[step], send_sem=a_s.at[step], recv_sem=a_r.at[step],
            device_id={"row": lax.rem(me + step, R)}, device_id_type=MESH,
        )

    def pack(buf, step):
        rows, valid = pair(me, lax.rem(me + step, R))
        for s in range(CAP):
            for k in range(KP):
                scale = jnp.where(valid, a_pat[k, rows[s]], 0).astype(jnp.float32)
                buf[step, s, k] = jnp.zeros((L, L), jnp.float32)
                buf[step, s, k, 0:B, 0:B] = a_v[rows[s], k] * scale

    def step_of(j):
        half = lax.div(j + 1, 2)
        return R // 2 + half * (1 - 2 * lax.rem(j, 2))

    load_a.wait()

    def send_step(j, carry):
        step = step_of(j)
        pack(asend, step)
        a_copy(step).start()
        return carry

    lax.fori_loop(0, R - 1, send_step, 0)
    pack(arecv, 0)
    stage[...] = jnp.zeros_like(stage)
    macc[...] = jnp.zeros_like(macc)
    load_s.wait()

    def work(step, arrives):
        source = lax.rem(me - step + R, R)
        rows, valid = pair(source, me)
        for s in range(CAP):
            g = jnp.where(valid, owner[source * W + rows[s]] - me * W, 0)

            def slab(b, carry):
                for h in range(2):
                    stage[2 * b + h, 0:B, 0:B] = s_v[g, pl.ds(2 * b + h, B, stride=NA), :]
                for h in range(2):
                    hi, lo = split(stage[2 * b + h])
                    sh[b, s * L : (s + 1) * L, h * L : (h + 1) * L] = hi
                    sl[b, s * L : (s + 1) * L, h * L : (h + 1) * L] = lo
                return carry

            lax.fori_loop(0, NA // 2, slab, 0)
        if arrives:
            a_copy(step).wait_recv()
        for s in range(CAP):
            for k in range(KP):
                hi, lo = split(arecv[step, s, k].T)
                ath[k * L : (k + 1) * L, s * L : (s + 1) * L] = hi
                atl[k * L : (k + 1) * L, s * L : (s + 1) * L] = lo

        def add(b, carry):
            r = mul3(ath[...], atl[...], sh[b], sl[b])
            macc[2 * b] += r[:, 0:L]
            macc[2 * b + 1] += r[:, L : 2 * L]
            return carry

        lax.fori_loop(0, NA // 2, add, 0)

    def remote_step(j, carry):
        work(step_of(j), True)
        return carry

    work(0, False)
    at = 0
    for t in range(1, Z):
        hop(t)
        until = (R - 1) * t // Z if t < Z - 1 else R - 1
        lax.fori_loop(at, until, remote_step, 0)
        at = until

    def m_copy(step):
        target = lax.rem(me + step, R)
        return pltpu.make_async_remote_copy(
            src_ref=macc.at[target], dst_ref=mrecv.at[step], send_sem=m_s.at[step], recv_sem=m_r.at[step],
            device_id={"row": target}, device_id_type=MESH,
        )

    def m_send(j, carry):
        m_copy(step_of(j)).start()
        return carry

    lax.fori_loop(0, R - 1, m_send, 0)

    for zo in range(Z):
        for i in range(1, Y):
            across(zo, i).wait_recv()

    def p_split(r, carry):
        for n in range(NJ):
            hi, lo = split(pbuf[r, n])
            at = pl.ds(pl.multiple_of(r * L, L), L)
            ph[at, n * L : (n + 1) * L] = hi
            plo[at, n * L : (n + 1) * L] = lo
        return carry

    lax.fori_loop(0, R, p_split, 0)

    mfull[col] = macc[me]

    def m_add(j, carry):
        step = step_of(j)
        m_copy(step).wait_recv()
        mfull[col] += mrecv[step]
        return carry

    lax.fori_loop(0, R - 1, m_add, 0)

    def g_copy(i):
        return pltpu.make_async_remote_copy(
            src_ref=mfull.at[col], dst_ref=mfull.at[col], send_sem=g_s.at[i], recv_sem=g_r.at[i],
            device_id={"col": lax.rem(col + i, C)}, device_id_type=MESH,
        )

    for i in range(1, C):
        g_copy(i).start()
    total[...] = jnp.zeros_like(total)

    for i in range(C):
        source = lax.rem(col - i + C, C)
        if i > 0:
            g_copy(i).wait_recv()
        for k in range(KP):
            hi, lo = split(mfull[source, k * L : (k + 1) * L, :].T)
            mth[:, k * L : (k + 1) * L] = hi
            mtl[:, k * L : (k + 1) * L] = lo
        rows = pl.ds(pl.multiple_of(source * KP * L, KP * L), KP * L)
        total[...] += mul3(mth[...], mtl[...], ph[rows, :], plo[rows, :])

    for n in range(NJ):
        out[0, n] = total[0:B, n * L : n * L + B]

    def a_done(j, carry):
        a_copy(j + 1).wait_send()
        m_copy(j + 1).wait_send()
        return carry

    lax.fori_loop(0, R - 1, a_done, 0)
    for i in range(1, C):
        g_copy(i).wait_send()
    for t in range(Z):
        @pl.when((z >= t) & (z < Z - 1))
        def _():
            up(t).wait_send()

        @pl.when((z + t < Z) & (z > 0))
        def _():
            down(t).wait_send()

    for zo in range(Z):
        for i in range(1, Y):
            across(zo, i).wait_send()


def shards(a_blocks, a_pattern, row_owner, prolong, p_pattern, prolong_slab):
    R, C = lax.axis_size("row"), lax.axis_size("col")
    W, KP, B = a_blocks.shape[:3]
    NA, NJ = prolong_slab.shape[1], prolong.shape[1]
    f32, bf16 = jnp.float32, jnp.bfloat16
    slab = prolong_slab.transpose(0, 2, 1, 3).reshape(W, B * NA, B)
    dma = pltpu.SemaphoreType.DMA
    vmem = pl.BlockSpec(memory_space=pltpu.VMEM)
    smem = pl.BlockSpec(memory_space=pltpu.SMEM)
    hbm = pl.BlockSpec(memory_space=pl.ANY)
    return pl.pallas_call(
        functools.partial(kernel, R, C),
        out_shape=jax.ShapeDtypeStruct((1, NJ, B, B), f32),
        in_specs=[hbm, hbm, vmem, smem, smem, smem],
        out_specs=vmem,
        scratch_shapes=[
            pltpu.VMEM((W, KP, B, B), f32),
            pltpu.VMEM((W, B * NA, B), f32),
            pltpu.VMEM((R, CAP, KP, L, L), f32),
            pltpu.VMEM((R, CAP, KP, L, L), f32),
            pltpu.VMEM((NA, L, L), f32),
            pltpu.VMEM((NA // 2, CAP * L, 2 * L), bf16),
            pltpu.VMEM((NA // 2, CAP * L, 2 * L), bf16),
            pltpu.VMEM((KP * L, CAP * L), bf16),
            pltpu.VMEM((KP * L, CAP * L), bf16),
            pltpu.VMEM((NA, KP * L, L), f32),
            pltpu.VMEM((R, KP * L, L), f32),
            pltpu.VMEM((C, KP * L, L), f32),
            pltpu.VMEM((L, KP * L), bf16),
            pltpu.VMEM((L, KP * L), bf16),
            pltpu.VMEM((R, NJ, L, L), f32),
            pltpu.VMEM((R * L, NJ * L), bf16),
            pltpu.VMEM((R * L, NJ * L), bf16),
            pltpu.VMEM((L, NJ * L), f32),
            dma((2,)),
            dma((R,)), dma((R,)), dma((R,)), dma((R,)), dma((C,)), dma((C,)),
            dma((Z,)), dma((Z + 1,)), dma((Z,)), dma((Z + 1,)), dma((R,)), dma((R,)),
        ],
        compiler_params=pltpu.CompilerParams(
            collective_id=0, has_side_effects=True, vmem_limit_bytes=58 * 1024 * 1024
        ),
    )(a_blocks, slab, prolong, row_owner, a_pattern.T, p_pattern)


def solution(mesh):
    in_specs = (
        P("row", "col", None, None),
        P("row", "col"),
        P(),
        P("row", "col", None, None),
        P("row", "col"),
        P("row", None, None, None),
    )
    out_specs = P("row", "col", None, None)
    return jax.shard_map(shards, mesh=mesh, in_specs=in_specs, out_specs=out_specs, check_vma=False)
```

```python
import functools

import jax
import jax.numpy as jnp
from jax import lax
from jax.experimental import pallas as pl
from jax.experimental.pallas import tpu as pltpu
from jax.sharding import PartitionSpec as P

CAP = 2
Z = 4
L = 128
MESH = pl.DeviceIdType.MESH


def split(v):
    hi = v.astype(jnp.bfloat16)
    lo = (v - hi.astype(jnp.float32)).astype(jnp.bfloat16)
    return hi, lo


def mul3(ah, al, bh, bl):
    dot = functools.partial(jnp.dot, preferred_element_type=jnp.float32)
    return dot(ah, bh) + (dot(ah, bl) + dot(al, bh))


def kernel(
    R, C, a_hbm, s_hbm, p_in, owner, a_pat, p_pat, out,
    a_v, s_v, asend, arecv, stage, sh, sl, ath, atl, macc, mrecv, mfull, mth, mtl, pbuf, ph, plo, total,
    load, a_s, a_r, m_s, m_r, g_s, g_r, u_s, u_r, d_s, d_r, y_s, y_r,
):
    W, KP, B = a_v.shape[0], a_v.shape[1], a_v.shape[2]
    NA, NJ = s_v.shape[1] // B, p_in.shape[0]
    Y = R // Z
    me, col = lax.axis_index("row"), lax.axis_index("col")
    z, y = lax.div(me, Y), lax.rem(me, Y)

    load_a = pltpu.make_async_copy(a_hbm, a_v, load.at[0])
    load_s = pltpu.make_async_copy(s_hbm, s_v, load.at[1])
    load_a.start()
    load_s.start()

    barrier = pltpu.get_barrier_semaphore()
    for i in range(1, R):
        pl.semaphore_signal(barrier, inc=1, device_id={"row": lax.rem(me + i, R)}, device_id_type=MESH)
    for i in range(1, C):
        pl.semaphore_signal(barrier, inc=1, device_id={"col": lax.rem(col + i, C)}, device_id_type=MESH)

    pl.semaphore_wait(barrier, R + C - 2)

    def p_copy(slot, target, s_sem, r_sem):
        return pltpu.make_async_remote_copy(
            src_ref=pbuf.at[slot], dst_ref=pbuf.at[slot], send_sem=s_sem, recv_sem=r_sem,
            device_id={"row": target}, device_id_type=MESH,
        )

    def up(t):
        return p_copy((z - t) * Y + y, me + Y, u_s.at[t], u_r.at[t + 1])

    def down(t):
        return p_copy((z + t) * Y + y, me - Y, d_s.at[t], d_r.at[t + 1])

    def across(zo, i):
        return p_copy(zo * Y + y, z * Y + lax.rem(y + i, Y), y_s.at[zo * Y + i], y_r.at[zo * Y + i])

    def hop(t):
        @pl.when(z >= t)
        def _():
            if t > 0:
                p_copy((z - t) * Y + y, me, u_s.at[t], u_r.at[t]).wait_recv()

            @pl.when(z < Z - 1)
            def _():
                up(t).start()

            for i in range(1, Y):
                across(z - t, i).start()

        @pl.when(z + t < Z)
        def _():
            if t > 0:
                p_copy((z + t) * Y + y, me, d_s.at[t], d_r.at[t]).wait_recv()

            @pl.when(z > 0)
            def _():
                down(t).start()

            if t > 0:
                for i in range(1, Y):
                    across(z + t, i).start()


    def pair(source, target):
        first, last = jnp.int32(W), jnp.int32(-1)
        for e in range(W):
            hit = lax.div(owner[source * W + e], W) == target
            first = jnp.minimum(first, jnp.where(hit, e, W))
            last = jnp.maximum(last, jnp.where(hit, e, -1))
        valid = last >= 0
        return (jnp.where(valid, first, 0), jnp.where(valid, last, 0)), valid

    def a_copy(step):
        return pltpu.make_async_remote_copy(
            src_ref=asend.at[step], dst_ref=arecv.at[step], send_sem=a_s.at[step], recv_sem=a_r.at[step],
            device_id={"row": lax.rem(me + step, R)}, device_id_type=MESH,
        )

    def pack(buf, step):
        rows, valid = pair(me, lax.rem(me + step, R))
        for s in range(CAP):
            for k in range(KP):
                scale = jnp.where(valid, a_pat[k, rows[s]], 0).astype(jnp.float32)
                buf[step, s, k] = jnp.zeros((L, L), jnp.float32)
                buf[step, s, k, 0:B, 0:B] = a_v[rows[s], k] * scale

    def step_of(j):
        half = lax.div(j + 1, 2)
        return R // 2 + half * (1 - 2 * lax.rem(j, 2))

    load_a.wait()

    def send_step(j, carry):
        step = step_of(j)
        pack(asend, step)
        a_copy(step).start()
        return carry

    lax.fori_loop(0, R - 1, send_step, 0)
    for n in range(NJ):
        pbuf[me, n] = jnp.zeros((L, L), jnp.float32)
        pbuf[me, n, 0:B, 0:B] = p_in[n, :, 0, :] * p_pat[0, n].astype(jnp.float32)
    hop(0)
    pack(arecv, 0)
    stage[...] = jnp.zeros_like(stage)
    macc[...] = jnp.zeros_like(macc)
    load_s.wait()

    def m_copy(step):
        target = lax.rem(me + step, R)
        return pltpu.make_async_remote_copy(
            src_ref=macc.at[target], dst_ref=mrecv.at[step], send_sem=m_s.at[step], recv_sem=m_r.at[step],
            device_id={"row": target}, device_id_type=MESH,
        )

    def work(step, arrives, last=False):
        source = lax.rem(me - step + R, R)
        rows, valid = pair(source, me)
        for s in range(CAP):
            g = jnp.where(valid, owner[source * W + rows[s]] - me * W, 0)

            def slab(b, carry):
                for h in range(2):
                    stage[2 * b + h, 0:B, 0:B] = s_v[g, pl.ds(2 * b + h, B, stride=NA), :]
                for h in range(2):
                    hi, lo = split(stage[2 * b + h])
                    sh[b, s * L : (s + 1) * L, h * L : (h + 1) * L] = hi
                    sl[b, s * L : (s + 1) * L, h * L : (h + 1) * L] = lo
                return carry

            lax.fori_loop(0, NA // 2, slab, 0)
        if arrives:
            a_copy(step).wait_recv()
        for s in range(CAP):
            for k in range(KP):
                hi, lo = split(arecv[step, s, k].T)
                ath[k * L : (k + 1) * L, s * L : (s + 1) * L] = hi
                atl[k * L : (k + 1) * L, s * L : (s + 1) * L] = lo

        def add(i, carry):
            b = lax.rem(i + lax.div(me, 2), NA // 2)
            r = mul3(ath[...], atl[...], sh[b], sl[b])
            macc[2 * b] += r[:, 0:L]
            macc[2 * b + 1] += r[:, L : 2 * L]
            for h in range(2 if last else 0):
                @pl.when(2 * b + h != me)
                def _():
                    m_copy(lax.rem(2 * b + h - me + R, R)).start()
            return carry

        lax.fori_loop(0, NA // 2, add, 0)

    def remote_step(j, carry):
        work(step_of(j), True)
        return carry

    work(0, False)
    at = 0
    for t in range(1, Z):
        hop(t)
        until = (R - 1) * t // Z if t < Z - 1 else R - 2
        lax.fori_loop(at, until, remote_step, 0)
        at = until
    work(step_of(jnp.int32(R - 2)), True, last=True)

    for zo in range(Z):
        for i in range(1, Y):
            across(zo, i).wait_recv()

    def p_split(r, carry):
        for n in range(NJ):
            hi, lo = split(pbuf[r, n])
            at = pl.ds(pl.multiple_of(r * L, L), L)
            ph[at, n * L : (n + 1) * L] = hi
            plo[at, n * L : (n + 1) * L] = lo
        return carry

    lax.fori_loop(0, R, p_split, 0)

    mfull[col] = macc[me]

    def m_add(j, carry):
        step = step_of(j)
        m_copy(step).wait_recv()
        mfull[col] += mrecv[step]
        return carry

    lax.fori_loop(0, R - 1, m_add, 0)

    def g_copy(i):
        return pltpu.make_async_remote_copy(
            src_ref=mfull.at[col], dst_ref=mfull.at[col], send_sem=g_s.at[i], recv_sem=g_r.at[i],
            device_id={"col": lax.rem(col + i, C)}, device_id_type=MESH,
        )

    for i in range(1, C):
        g_copy(i).start()
    total[...] = jnp.zeros_like(total)

    for i in range(C):
        source = lax.rem(col - i + C, C)
        if i > 0:
            g_copy(i).wait_recv()
        for k in range(KP):
            hi, lo = split(mfull[source, k * L : (k + 1) * L, :].T)
            mth[:, k * L : (k + 1) * L] = hi
            mtl[:, k * L : (k + 1) * L] = lo
        rows = pl.ds(pl.multiple_of(source * KP * L, KP * L), KP * L)
        total[...] += mul3(mth[...], mtl[...], ph[rows, :], plo[rows, :])

    for n in range(NJ):
        out[0, n] = total[0:B, n * L : n * L + B]

    def a_done(j, carry):
        a_copy(j + 1).wait_send()
        m_copy(j + 1).wait_send()
        return carry

    lax.fori_loop(0, R - 1, a_done, 0)
    for i in range(1, C):
        g_copy(i).wait_send()
    for t in range(Z):
        @pl.when((z >= t) & (z < Z - 1))
        def _():
            up(t).wait_send()

        @pl.when((z + t < Z) & (z > 0))
        def _():
            down(t).wait_send()

    for zo in range(Z):
        for i in range(1, Y):
            across(zo, i).wait_send()


def shards(a_blocks, a_pattern, row_owner, prolong, p_pattern, prolong_slab):
    R, C = lax.axis_size("row"), lax.axis_size("col")
    W, KP, B = a_blocks.shape[:3]
    NA, NJ = prolong_slab.shape[1], prolong.shape[1]
    f32, bf16 = jnp.float32, jnp.bfloat16
    slab = prolong_slab.transpose(0, 2, 1, 3).reshape(W, B * NA, B)
    dma = pltpu.SemaphoreType.DMA
    vmem = pl.BlockSpec(memory_space=pltpu.VMEM)
    smem = pl.BlockSpec(memory_space=pltpu.SMEM)
    hbm = pl.BlockSpec(memory_space=pl.ANY)
    return pl.pallas_call(
        functools.partial(kernel, R, C),
        out_shape=jax.ShapeDtypeStruct((1, NJ, B, B), f32),
        in_specs=[hbm, hbm, vmem, smem, smem, smem],
        out_specs=vmem,
        scratch_shapes=[
            pltpu.VMEM((W, KP, B, B), f32),
            pltpu.VMEM((W, B * NA, B), f32),
            pltpu.VMEM((R, CAP, KP, L, L), f32),
            pltpu.VMEM((R, CAP, KP, L, L), f32),
            pltpu.VMEM((NA, L, L), f32),
            pltpu.VMEM((NA // 2, CAP * L, 2 * L), bf16),
            pltpu.VMEM((NA // 2, CAP * L, 2 * L), bf16),
            pltpu.VMEM((KP * L, CAP * L), bf16),
            pltpu.VMEM((KP * L, CAP * L), bf16),
            pltpu.VMEM((NA, KP * L, L), f32),
            pltpu.VMEM((R, KP * L, L), f32),
            pltpu.VMEM((C, KP * L, L), f32),
            pltpu.VMEM((L, KP * L), bf16),
            pltpu.VMEM((L, KP * L), bf16),
            pltpu.VMEM((R, NJ, L, L), f32),
            pltpu.VMEM((R * L, NJ * L), bf16),
            pltpu.VMEM((R * L, NJ * L), bf16),
            pltpu.VMEM((L, NJ * L), f32),
            dma((2,)),
            dma((R,)), dma((R,)), dma((R,)), dma((R,)), dma((C,)), dma((C,)),
            dma((Z,)), dma((Z + 1,)), dma((Z,)), dma((Z + 1,)), dma((R,)), dma((R,)),
        ],
        compiler_params=pltpu.CompilerParams(
            collective_id=0, has_side_effects=True, vmem_limit_bytes=58 * 1024 * 1024
        ),
    )(a_blocks, slab, prolong.transpose(1, 2, 0, 3), row_owner, a_pattern.T, p_pattern)


def solution(mesh):
    in_specs = (
        P("row", "col", None, None),
        P("row", "col"),
        P(),
        P("row", "col", None, None),
        P("row", "col"),
        P("row", None, None, None),
    )
    out_specs = P("row", "col", None, None)
    return jax.shard_map(shards, mesh=mesh, in_specs=in_specs, out_specs=out_specs, check_vma=False)
```
